32 devices in a mesh: dp: 8 (over z, x), tensor: 4 (over y, core).
Axes of the slice: x: 2, y: 2, z: 4, core: 2. Of those that a mesh axis runs over, the one named last changes fastest.
Arguments:
- normed_hidden_state: bfloat16 [4, 512, 8192], P(None, 'dp', 'tensor'), may hold values from -6 to 6
- query_projection_weight: bfloat16 [8192, 4096], P(None, 'tensor'), may hold values from -0.0625 to 0.0625
- adapter_down_maps: bfloat16 [1024, 8192], P('dp', 'tensor'), may hold values from -0.0625 to 0.0625
- adapter_up_maps: bfloat16 [1024, 4096], P('dp', 'tensor'), may hold values from -0.75 to 0.75
- key_value_cache: bfloat16 [2, 512, 128, 512], P(None, 'dp', None, 'tensor'), may hold values from -82 to 82
- step_key_value: bfloat16 [4, 2, 512, 512], P(None, None, 'dp', 'tensor'), may hold values from -6 to 6
- cache_valid_length: int32 [512], P('dp'), may hold values from 1 to 128, as said below
- adapter_per_request: int32 [512], P('dp'), may hold values from 0 to 15, as said below
- adapter_pool_position: int32 [16], replicated, may hold values from 0 to 15, as said below
Outputs:
- attended: bfloat16 [4, 512, 4096], P(None, 'dp', 'tensor')
The draws below stay inside these ranges and needn't reach their ends.
Inputs may be any that keep to these rules, and one draw needn't show every extreme that they name: `adapter_pool_position`: A permutation: every adapter has its own pool position, and position p is held by dp index p // 2. `adapter_per_request`: within each group of 64 consecutive requests, requests whose adapters sit on the same dp index use the same adapter; some dp index serves an adapter to every group. `cache_valid_length`: each group of 64 consecutive requests holds a request with all 128 positions valid.
All inputs are finite; a program needn't handle non-finite values.
Results may differ from the reference program's by a relative error of at most 0.015.
Values may be sent and summed in bfloat16 or wider, within the bound.
A program may use at most 192 MiB of HBM per device.

```python
import math
import jax
import jax.numpy as jnp
from jax import lax

MODEL_WIDTH = 8192
HEADS = 32
KV_HEADS = 4
HEAD_SIZE = 128
ADAPTER_RANK = 64
STEPS = 4
POOL_DEV = 2
REQ_GRP = 64
CACHE = 128
QUERY_FEATURES = 4096
KVW = 512
REQS = 512
ADAPTER_POOL = 16


def pool_order(key):
    return jax.random.permutation(jax.random.fold_in(key, 11), ADAPTER_POOL).astype(jnp.int32)


def draw_adapter_pool_position(key, part):
    return pool_order(key)


def draw_adapter_per_request(key, part):
    groups = REQS // REQ_GRP
    order = pool_order(key)
    inverse = jnp.argsort(order).astype(jnp.int32)
    owner = jax.random.randint(jax.random.fold_in(key, 12), (groups, REQ_GRP), 0, groups).astype(jnp.int32)
    common = jax.random.randint(jax.random.fold_in(key, 13), (), 0, groups).astype(jnp.int32)
    chosen = jax.random.randint(jax.random.fold_in(key, 14), (groups,), 0, REQ_GRP).astype(jnp.int32)
    owner = jnp.where(jnp.arange(REQ_GRP, dtype=jnp.int32)[None, :] == chosen[:, None], common, owner)
    slot_table = jax.random.randint(jax.random.fold_in(key, 15), (groups, groups), 0, POOL_DEV).astype(jnp.int32)
    picked = jnp.take_along_axis(slot_table, owner, axis=1)
    spot = owner * POOL_DEV + picked
    return jnp.take(inverse, spot.reshape(-1), axis=0).astype(jnp.int32)


def draw_cache_valid_length(key, part):
    groups = REQS // REQ_GRP
    lengths = jax.random.randint(jax.random.fold_in(key, 21), (groups, REQ_GRP), 1, CACHE + 1).astype(jnp.int32)
    chosen = jax.random.randint(jax.random.fold_in(key, 22), (groups,), 0, REQ_GRP).astype(jnp.int32)
    lengths = jnp.where(jnp.arange(REQ_GRP, dtype=jnp.int32)[None, :] == chosen[:, None], CACHE, lengths)
    return lengths.reshape(-1).astype(jnp.int32)


def draw_key_value_cache(key, part):
    shape = (2, REQS, CACHE, KVW)
    result = jnp.clip(jax.random.normal(jax.random.fold_in(key, 34), shape, jnp.float32), -4.0, 4.0)
    return result.astype(jnp.bfloat16)


def block_levels(own_key, dims, pieces, low, top_value):
    factor_of = 1.0
    for dim, shards_of in pieces:
        steps = jax.random.uniform(jax.random.fold_in(jax.random.fold_in(own_key, 6), dim), (shards_of,), jnp.float32, low / len(pieces), top_value / len(pieces))
        factor_of = factor_of * jnp.repeat(jnp.exp(steps), dims[dim] // shards_of).reshape((-1,) + (1,) * (len(dims) - 1 - dim))
    return factor_of


def scatter_about(rng, shape, scale, limit, pieces=(), kind=jnp.bfloat16):
    entries = jax.random.normal(rng, shape, jnp.float32) * scale
    if len(pieces) > 0:
        entries = block_levels(rng, shape, pieces, -0.22, 0.18) * entries
    return jnp.clip(entries, min=-limit, max=limit).astype(kind)


def setup_inputs(seed: int = 0) -> dict:
    key_of = jax.random.split(jax.random.key(seed), 10)
    return {
        "normed_hidden_state": scatter_about(key_of[0], (STEPS, REQS, MODEL_WIDTH), 1.0, 6.0, ((1, 8), (2, 4))),
        "query_projection_weight": scatter_about(key_of[1], (MODEL_WIDTH, QUERY_FEATURES), MODEL_WIDTH ** -0.5, 0.0625, ((1, 4),)),
        "adapter_down_maps": scatter_about(key_of[2], (ADAPTER_POOL * ADAPTER_RANK, MODEL_WIDTH), MODEL_WIDTH ** -0.5, 0.0625, ((0, 8), (1, 4))),
        "adapter_up_maps": scatter_about(key_of[3], (ADAPTER_POOL * ADAPTER_RANK, QUERY_FEATURES), ADAPTER_RANK ** -0.5, 0.75, ((0, 8), (1, 4))),
        "key_value_cache": draw_key_value_cache(jax.random.fold_in(key_of[9], 71), 0),
        "step_key_value": scatter_about(key_of[5], (STEPS, 2, REQS, KVW), 1.0, 6.0, ((2, 8), (3, 4))),
        "cache_valid_length": draw_cache_valid_length(jax.random.fold_in(key_of[9], 71), 0),
        "adapter_per_request": draw_adapter_per_request(jax.random.fold_in(key_of[9], 71), 0),
        "adapter_pool_position": draw_adapter_pool_position(jax.random.fold_in(key_of[9], 71), 0),
    }


def reference(normed_hidden_state, query_projection_weight, adapter_down_maps, adapter_up_maps, key_value_cache, step_key_value, cache_valid_length, adapter_per_request, adapter_pool_position):
    position = jnp.take(adapter_pool_position, adapter_per_request, axis=0).astype(jnp.int32)
    token_rows = normed_hidden_state.reshape(STEPS * REQS, MODEL_WIDTH)
    base = jnp.dot(token_rows, query_projection_weight, preferred_element_type=jnp.float32).reshape(STEPS, REQS, QUERY_FEATURES)
    down_map_pages = adapter_down_maps.reshape(ADAPTER_POOL, ADAPTER_RANK, MODEL_WIDTH)
    up_map_pages = adapter_up_maps.reshape(ADAPTER_POOL, ADAPTER_RANK, QUERY_FEATURES)

    def adapt_one(item):
        request_rows, spot = item
        down_page = down_map_pages[spot]
        up_page = up_map_pages[spot]
        shrink = lax.dot_general(request_rows, down_page, (((1,), (1,)), ((), ())), preferred_element_type=jnp.float32)
        shrink = shrink.astype(jnp.bfloat16)
        return jnp.dot(shrink, up_page, preferred_element_type=jnp.float32)
    delta = lax.map(adapt_one, (jnp.transpose(normed_hidden_state, (1, 0, 2)), position))
    query = (base + jnp.transpose(delta, (1, 0, 2))).astype(jnp.bfloat16)
    group = HEADS // KV_HEADS
    scale = 1.0 / math.sqrt(HEAD_SIZE)
    grouped = query.astype(jnp.float32).reshape(STEPS, REQS, KV_HEADS, group, HEAD_SIZE)
    keys = key_value_cache[0].astype(jnp.float32).reshape(REQS, CACHE, KV_HEADS, HEAD_SIZE)
    values = key_value_cache[1].astype(jnp.float32).reshape(REQS, CACHE, KV_HEADS, HEAD_SIZE)
    new_keys = step_key_value[:, 0].astype(jnp.float32).reshape(STEPS, REQS, KV_HEADS, HEAD_SIZE)
    new_values = step_key_value[:, 1].astype(jnp.float32).reshape(STEPS, REQS, KV_HEADS, HEAD_SIZE)
    cache_scores = jnp.einsum('trkgd,rckd->trkgc', grouped, keys) * scale
    valid = jnp.arange(CACHE, dtype=jnp.int32)[None, :] < cache_valid_length[:, None]
    cache_scores = jnp.where(valid[None, :, None, None, :], cache_scores, -1e+30)
    fresh_scores = jnp.einsum('trkgd,srkd->trkgs', grouped, new_keys) * scale
    causal = jnp.arange(STEPS, dtype=jnp.int32)[:, None] >= jnp.arange(STEPS, dtype=jnp.int32)[None, :]
    fresh_scores = jnp.where(causal[:, None, None, None, :], fresh_scores, -1e+30)
    top = jnp.maximum(lax.optimization_barrier(jnp.max(cache_scores, axis=-1)), lax.optimization_barrier(jnp.max(fresh_scores, axis=-1)))
    cache_expo = jnp.exp(cache_scores - top[..., None])
    fresh_expo = jnp.exp(fresh_scores - top[..., None])
    total = lax.optimization_barrier(jnp.sum(cache_expo, axis=-1)) + lax.optimization_barrier(jnp.sum(fresh_expo, axis=-1))
    cache_weights = lax.optimization_barrier(cache_expo.astype(jnp.bfloat16)).astype(jnp.float32)
    fresh_weights = lax.optimization_barrier(fresh_expo.astype(jnp.bfloat16)).astype(jnp.float32)
    mixed = jnp.einsum('trkgc,rckd->trkgd', cache_weights, values)
    mixed = mixed + jnp.einsum('trkgs,srkd->trkgd', fresh_weights, new_values)
    attended = mixed / total[..., None]
    return attended.reshape(STEPS, REQS, QUERY_FEATURES).astype(jnp.bfloat16)
```

```python
import functools
import math

import jax
import jax.numpy as jnp
from jax import lax
from jax.experimental import pallas as pl
from jax.experimental.pallas import tpu as pltpu
from jax.sharding import PartitionSpec as P

HEAD_SIZE = 128
ADAPTER_RANK = 64
MESH = pl.DeviceIdType.MESH
F32 = jnp.float32
BF16 = jnp.bfloat16


def project_kernel(
    line,
    hid_hbm,
    w_hbm,
    down_hbm,
    up_hbm,
    pos_hbm,
    query_ref,
    hid,
    rows_x,
    pos,
    downs,
    ups,
    w,
    acc,
    part,
    got,
    local_sem,
    w_sem,
    h1_s,
    h1_r,
    h2_s,
    h2_r,
    hf_s,
    hf_r,
    x_s,
    x_r,
    zd_s,
    zd_r,
    zu_s,
    zu_r,
    xu_s,
    xu_r,
    red_s,
    red_r,
):
    d = lax.axis_index("dp")
    t = lax.axis_index("tensor")
    q, p = d // 2, d % 2
    other = 1 - p
    t1 = t + 1 - 2 * (t % 2)
    t2 = (t + 2) % 4
    t3 = (t1 + 2) % 4
    above, below, across = (d + 2, t), (d - 2, t), (d + 1 - 2 * p, t)
    side1, side2 = (d, t1), (d, t2)
    count = hid.shape[1]
    width = hid.shape[2]
    chunk = count // 4
    out_cols = w.shape[1]
    has_above, has_below = q < line - 1, q > 0

    def local(src, dst, k):
        return pltpu.make_async_copy(src, dst, local_sem.at[k])

    def remote(src, dst, s, r, to):
        return pltpu.make_async_remote_copy(
            src_ref=src, dst_ref=dst, send_sem=s, recv_sem=r, device_id=to, device_id_type=MESH
        )

    first = [
        local(down_hbm, downs.at[q], 0),
        local(hid_hbm, hid.at[t], 1),
        local(pos_hbm, pos.at[0], 2),
        local(up_hbm, ups.at[p, q], 3),
    ]
    for c in first:
        c.start()
    order = [t, t1, t2, t3]
    w_copies = []
    for k, block in enumerate(order):
        span = pl.ds(pl.multiple_of(block * width, width), width)
        w_copies.append(pltpu.make_async_copy(w_hbm.at[span], w.at[span], w_sem.at[k]))
        w_copies[-1].start()

    barrier = pltpu.get_barrier_semaphore()
    for peer in (across, side1, side2):
        pl.semaphore_signal(barrier, inc=1, device_id=peer, device_id_type=MESH)

    @pl.when(has_above)
    def _():
        pl.semaphore_signal(barrier, inc=1, device_id=above, device_id_type=MESH)

    @pl.when(has_below)
    def _():
        pl.semaphore_signal(barrier, inc=1, device_id=below, device_id_type=MESH)

    pl.semaphore_wait(
        barrier, 3 + jnp.where(has_above, 1, 0) + jnp.where(has_below, 1, 0)
    )
    for c in first:
        c.wait()

    def line_copy(kind, way, s, slot):
        ref = downs.at[slot] if kind == 0 else ups.at[p, slot]
        send, recv = (zd_s, zd_r) if kind == 0 else (zu_s, zu_r)
        return remote(
            ref, ref, send.at[way, s], recv.at[way, s], above if way == 0 else below
        )

    def sends(way, s):
        if way == 0:
            return jnp.logical_and(has_above, q - s >= 0)
        return jnp.logical_and(has_below, q + s <= line - 1)

    def sent_slot(way, s):
        return q - s if way == 0 else q + s

    def arrives(way, s):
        return q - 1 - s >= 0 if way == 0 else q + 1 + s <= line - 1

    def arrived_slot(way, s):
        return q - 1 - s if way == 0 else q + 1 + s

    def send_line(kind, way, s):
        @pl.when(sends(way, s))
        def _():
            line_copy(kind, way, s, sent_slot(way, s)).start()

    def cross_copy(index, slot, parity):
        ref = ups.at[parity, slot]
        return remote(ref, ref, xu_s.at[index], xu_r.at[index], across)

    x_rows = remote(hid.at[t], rows_x, x_s.at[0], x_r.at[0], across)
    x_pos = remote(pos.at[0], pos.at[1], x_s.at[1], x_r.at[1], across)
    to1 = remote(hid.at[t], hid.at[t], h1_s, h1_r, side1)

    def part_of(block, c):
        return hid.at[block, pl.ds(c * chunk, chunk)]

    to2 = [
        remote(part_of(t, c), part_of(t, c), h2_s.at[c], h2_r.at[c], side2) for c in range(4)
    ]
    from2 = [
        remote(part_of(t2, c), part_of(t2, c), h2_s.at[c], h2_r.at[c], side2) for c in range(4)
    ]
    on1 = [
        remote(part_of(t2, c), part_of(t2, c), hf_s.at[c], hf_r.at[c], side1) for c in range(4)
    ]
    by1 = [
        remote(part_of(t3, c), part_of(t3, c), hf_s.at[c], hf_r.at[c], side1) for c in range(4)
    ]
    send_line(0, 0, 0)
    send_line(0, 1, 0)
    for c in to2:
        c.start()
    x_pos.start()
    x_rows.start()
    to1.start()
    send_line(1, 0, 0)
    send_line(1, 1, 0)
    cross_copy(q, q, p).start()

    tile = 256

    def base(block, k, start):
        w_copies[k].wait()
        span = pl.ds(pl.multiple_of(block * width, width), width)

        @pl.loop(0, out_cols // tile)
        def _(n):
            cols = pl.ds(pl.multiple_of(n * tile, tile), tile)
            value = jnp.dot(hid[block], w[span, cols], preferred_element_type=F32)
            if start:
                acc[:, cols] = value
            else:
                acc[:, cols] += value

    half = lax.broadcasted_iota(jnp.int32, (count // 4, 2 * ADAPTER_RANK), 1) // ADAPTER_RANK

    def keep(which, wanted):
        m = jnp.where(wanted, 1, 0)
        return jnp.concatenate([m] * 4, axis=0) > 0

    def shrink(which, slot, start=False):
        source = hid[t] if which == 0 else rows_x[...]
        value = lax.dot_general(
            source, downs[slot], (((1,), (1,)), ((), ())), preferred_element_type=F32
        )
        value = jnp.where(
            keep(which, pos[which] == 2 * (2 * slot + p) + half), value, 0.0
        )
        if start:
            part[which] = value
        else:
            part[which] += value

    base(t, 0, True)
    shrink(0, q, True)

    def pass_on(c):
        from2[c].wait_recv()
        on1[c].start()

    def down_step(s):
        for way in (0, 1):

            @pl.when(arrives(way, s))
            def _():
                line_copy(0, way, s, arrived_slot(way, s)).wait_recv()

            if s + 1 < line:
                send_line(0, way, s + 1)

    def down_use(which, s):
        for way in (0, 1):

            @pl.when(arrives(way, s))
            def _():
                shrink(which, arrived_slot(way, s))

    def up_step(s):
        for way in (0, 1):

            @pl.when(arrives(way, s))
            def _():
                slot = arrived_slot(way, s)
                line_copy(1, way, s, slot).wait_recv()
                cross_copy(slot, slot, p).start()

            if s + 1 < line:
                send_line(1, way, s + 1)

    pass_on(0)
    pass_on(1)
    down_step(0)
    down_use(0, 0)
    pass_on(2)
    up_step(0)
    pass_on(3)
    to1.wait_recv()
    base(t1, 1, False)
    x_pos.wait_recv()
    x_rows.wait_recv()
    shrink(1, q, True)
    down_use(1, 0)
    base(t2, 2, False)
    for s in range(1, line - 1):
        down_step(s)
        down_use(0, s)
        down_use(1, s)
        if s == 1:
            for c in by1:
                c.wait_recv()
            base(t3, 3, False)
        if s < line - 2:
            up_step(s)

    to_x = remote(part.at[1], got.at[0], red_s.at[0], red_r.at[0], across)
    to_x.start()
    to_x.wait_recv()
    part[0] += got[0]
    to_1 = remote(part.at[0], got.at[1], red_s.at[1], red_r.at[1], side1)
    to_1.start()
    to_1.wait_recv()
    part[2] = part[0] + got[1]
    to_2 = remote(part.at[2], got.at[2], red_s.at[2], red_r.at[2], side2)
    to_2.start()
    up_step(line - 2)
    to_2.wait_recv()
    total = (part[2] + got[2]).astype(BF16)

    def expand(parity, last):
        picked = jnp.concatenate(
            [
                jnp.where(keep(0, pos[0] // 2 == 2 * slot + parity), total, jnp.zeros_like(total))
                for slot in range(line)
            ],
            axis=1,
        )

        @pl.loop(0, out_cols // tile)
        def _(n):
            cols = pl.ds(pl.multiple_of(n * tile, tile), tile)
            maps = ups[parity, :, :, cols].reshape(line * 2 * ADAPTER_RANK, tile)
            value = acc[:, cols] + jnp.dot(picked, maps, preferred_element_type=F32)
            if last:
                query_ref[:, cols] = value.astype(BF16)
            else:
                acc[:, cols] = value

    expand(p, False)
    for slot in range(line):
        cross_copy(slot, slot, other).wait_recv()
    expand(other, True)

    x_rows.wait_send()
    x_pos.wait_send()
    to1.wait_send()
    for c in to2 + on1:
        c.wait_send()
    for c in (to_x, to_1, to_2):
        c.wait_send()
    for slot in range(line):
        cross_copy(slot, slot, p).wait_send()
    for s in range(line):
        for way in (0, 1):

            @pl.when(sends(way, s))
            def _():
                slot = sent_slot(way, s)
                line_copy(0, way, s, slot).wait_send()
                line_copy(1, way, s, slot).wait_send()


def project(token_rows, weight, down, up, position, line):
    count, width = token_rows.shape
    cols = weight.shape[1]
    pages = 2 * ADAPTER_RANK
    anywhere = pl.BlockSpec(memory_space=pl.ANY)
    sems = pltpu.SemaphoreType.DMA
    return pl.pallas_call(
        functools.partial(project_kernel, line),
        out_shape=jax.ShapeDtypeStruct((count, cols), BF16),
        in_specs=[anywhere] * 5,
        out_specs=pl.BlockSpec(memory_space=pltpu.VMEM),
        scratch_shapes=[
            pltpu.VMEM((4, count, width), BF16),
            pltpu.VMEM((count, width), BF16),
            pltpu.VMEM((2, count // 4, pages), jnp.int32),
            pltpu.VMEM((line, pages, width), BF16),
            pltpu.VMEM((2, line, pages, cols), BF16),
            pltpu.VMEM(weight.shape, BF16),
            pltpu.VMEM((count, cols), F32),
            pltpu.VMEM((3, count, pages), F32),
            pltpu.VMEM((3, count, pages), F32),
            sems((4,)),
            sems((4,)),
            sems,
            sems,
            sems((4,)),
            sems((4,)),
            sems((4,)),
            sems((4,)),
            sems((2,)),
            sems((2,)),
            sems((2, line)),
            sems((2, line)),
            sems((2, line)),
            sems((2, line)),
            sems((line,)),
            sems((line,)),
            sems((3,)),
            sems((3,)),
        ],
        compiler_params=pltpu.CompilerParams(
            collective_id=0, has_side_effects=True, vmem_limit_bytes=56 * 2**20
        ),
    )(token_rows, weight, down, up, position)


def attend_kernel(steps, q_ref, k_ref, v_ref, nk_ref, nv_ref, len_ref, out_ref):
    q = q_ref[...]
    scale = 1.0 / math.sqrt(HEAD_SIZE)
    dims = (((2,), (2,)), ((0,), (0,)))
    cached = lax.dot_general(q, k_ref[0], dims, preferred_element_type=F32) * scale
    fresh = lax.dot_general(q, nk_ref[...], dims, preferred_element_type=F32) * scale
    place = lax.broadcasted_iota(jnp.int32, cached.shape, 2)
    cached = jnp.where(place < len_ref[...], cached, -1e30)
    step = lax.broadcasted_iota(jnp.int32, fresh.shape, 1) // (q.shape[1] // steps)
    fresh = jnp.where(lax.broadcasted_iota(jnp.int32, fresh.shape, 2) <= step, fresh, -1e30)
    top = jnp.maximum(
        jnp.max(cached, axis=-1, keepdims=True), jnp.max(fresh, axis=-1, keepdims=True)
    )
    cached = jnp.exp(cached - top)
    fresh = jnp.exp(fresh - top)
    total = jnp.sum(cached, axis=-1, keepdims=True) + jnp.sum(fresh, axis=-1, keepdims=True)
    dims = (((2,), (1,)), ((0,), (0,)))
    mixed = lax.dot_general(cached.astype(BF16), v_ref[0], dims, preferred_element_type=F32)
    mixed += lax.dot_general(fresh.astype(BF16), nv_ref[...], dims, preferred_element_type=F32)
    out_ref[...] = (mixed / total).astype(BF16)


def attend(query, cache, fresh, lengths, steps):
    requests, rows, size = query.shape
    length = cache.shape[2]
    pad = fresh.shape[2]
    block = 8

    def spec(which, n):
        return pl.BlockSpec((1, block, n, size), lambda i: (which, i, 0, 0))

    def plain(n):
        return pl.BlockSpec((block, n, size), lambda i: (i, 0, 0))

    return pl.pallas_call(
        functools.partial(attend_kernel, steps),
        grid=(requests // block,),
        out_shape=jax.ShapeDtypeStruct(query.shape, BF16),
        in_specs=[
            plain(rows),
            spec(0, length),
            spec(1, length),
            plain(pad),
            plain(pad),
            plain(1),
        ],
        out_specs=plain(rows),
        compiler_params=pltpu.CompilerParams(vmem_limit_bytes=32 * 2**20),
    )(query, cache, cache, fresh[0], fresh[1], lengths)


def per_device(line, hidden, weight, down, up, cache, step_kv, valid, adapters, pool):
    steps, requests, width = hidden.shape
    table = jnp.arange(pool.shape[0], dtype=jnp.int32)
    position = jnp.sum(jnp.where(adapters[:, None] == table[None, :], pool[None, :], 0), axis=1)
    position = jnp.broadcast_to(position[:, None], (requests, 2 * ADAPTER_RANK))
    query = project(hidden.reshape(steps * requests, width), weight, down, up, position, line)
    heads = weight.shape[1] // HEAD_SIZE
    query = query.reshape(steps, requests, heads, HEAD_SIZE).transpose(1, 0, 2, 3)
    fresh = jnp.pad(step_kv.transpose(1, 2, 0, 3), ((0, 0), (0, 0), (0, 16 - steps), (0, 0)))
    lengths = jnp.broadcast_to(valid[:, None, None], (requests, 1, HEAD_SIZE))
    out = attend(
        query.reshape(requests, steps * heads, HEAD_SIZE), cache, fresh, lengths, steps
    )
    out = out.reshape(requests, steps, heads * HEAD_SIZE)
    return out.transpose(1, 0, 2)


def solution(mesh):
    return jax.shard_map(
        functools.partial(per_device, mesh.shape["dp"] // 2),
        mesh=mesh,
        in_specs=(
            P(None, "dp", "tensor"),
            P(None, "tensor"),
            P("dp", "tensor"),
            P("dp", "tensor"),
            P(None, "dp", None, "tensor"),
            P(None, None, "dp", "tensor"),
            P("dp"),
            P("dp"),
            P(),
        ),
        out_specs=P(None, "dp", "tensor"),
        check_vma=False,
    )
```

```python
import functools
import math

import jax
import jax.numpy as jnp
from jax import lax
from jax.experimental import pallas as pl
from jax.experimental.pallas import tpu as pltpu
from jax.sharding import PartitionSpec as P

HEAD_SIZE = 128
ADAPTER_RANK = 64
MESH = pl.DeviceIdType.MESH
F32 = jnp.float32
BF16 = jnp.bfloat16


def project_kernel(
    line,
    hid_hbm,
    w_hbm,
    down_hbm,
    up_hbm,
    pos_hbm,
    query_ref,
    hid,
    rows_x,
    pos,
    downs,
    ups,
    picks,
    ups_x,
    w,
    acc,
    part,
    packed,
    got,
    local_sem,
    w_sem,
    h1_s,
    h1_r,
    h2_s,
    h2_r,
    hf_s,
    hf_r,
    x_s,
    x_r,
    zd_s,
    zd_r,
    zu_s,
    zu_r,
    xu_s,
    xu_r,
    red_s,
    red_r,
):
    d = lax.axis_index("dp")
    t = lax.axis_index("tensor")
    q, p = d // 2, d % 2
    other = 1 - p
    t1 = t + 1 - 2 * (t % 2)
    t2 = (t + 2) % 4
    t3 = (t1 + 2) % 4
    above, below, across = (d + 2, t), (d - 2, t), (d + 1 - 2 * p, t)
    side1, side2 = (d, t1), (d, t2)
    count = hid.shape[1]
    width = hid.shape[2]
    chunk = count // 4
    out_cols = w.shape[1]
    has_above, has_below = q < line - 1, q > 0

    def local(src, dst, k):
        return pltpu.make_async_copy(src, dst, local_sem.at[k])

    def remote(src, dst, s, r, to):
        return pltpu.make_async_remote_copy(
            src_ref=src, dst_ref=dst, send_sem=s, recv_sem=r, device_id=to, device_id_type=MESH
        )

    first = [
        local(down_hbm, downs.at[q], 0),
        local(hid_hbm, hid.at[t], 1),
        local(pos_hbm, pos.at[0], 2),
        local(up_hbm, ups.at[q], 3),
    ]
    for c in first:
        c.start()
    order = [t, t1, t2, t3]
    w_copies = []
    for k, block in enumerate(order):
        span = pl.ds(pl.multiple_of(block * width, width), width)
        w_copies.append(pltpu.make_async_copy(w_hbm.at[span], w.at[span], w_sem.at[k]))
        w_copies[-1].start()

    barrier = pltpu.get_barrier_semaphore()
    for peer in (across, side1, side2):
        pl.semaphore_signal(barrier, inc=1, device_id=peer, device_id_type=MESH)

    @pl.when(has_above)
    def _():
        pl.semaphore_signal(barrier, inc=1, device_id=above, device_id_type=MESH)

    @pl.when(has_below)
    def _():
        pl.semaphore_signal(barrier, inc=1, device_id=below, device_id_type=MESH)

    pl.semaphore_wait(
        barrier, 3 + jnp.where(has_above, 1, 0) + jnp.where(has_below, 1, 0)
    )
    for c in first:
        c.wait()

    def line_copy(kind, way, s, slot):
        ref = downs.at[slot] if kind == 0 else ups.at[slot]
        send, recv = (zd_s, zd_r) if kind == 0 else (zu_s, zu_r)
        return remote(
            ref, ref, send.at[way, s], recv.at[way, s], above if way == 0 else below
        )

    def sends(way, s):
        if way == 0:
            return jnp.logical_and(has_above, q - s >= 0)
        return jnp.logical_and(has_below, q + s <= line - 1)

    def sent_slot(way, s):
        return q - s if way == 0 else q + s

    def arrives(way, s):
        return q - 1 - s >= 0 if way == 0 else q + 1 + s <= line - 1

    def arrived_slot(way, s):
        return q - 1 - s if way == 0 else q + 1 + s

    def send_line(kind, way, s):
        @pl.when(sends(way, s))
        def _():
            line_copy(kind, way, s, sent_slot(way, s)).start()

    def cross_copy(slot):
        return remote(picks.at[slot], ups_x.at[slot], xu_s.at[slot], xu_r.at[slot], across)

    def cross(slot):
        second = jnp.where(pos[1] == 2 * (2 * slot + p) + 1, 1.0, 0.0)
        second = jnp.max(second, axis=0, keepdims=True)
        second = jnp.broadcast_to(second, (ADAPTER_RANK, second.shape[1])) > 0.5
        for c in range(0, out_cols, 2 * ADAPTER_RANK):
            cols = pl.ds(c, 2 * ADAPTER_RANK)
            picks[slot, :, cols] = jnp.where(
                second,
                ups[slot, pl.ds(ADAPTER_RANK, ADAPTER_RANK), cols],
                ups[slot, pl.ds(0, ADAPTER_RANK), cols],
            )
        cross_copy(slot).start()

    x_rows = remote(hid.at[t], rows_x, x_s.at[0], x_r.at[0], across)
    x_pos = remote(pos.at[0], pos.at[1], x_s.at[1], x_r.at[1], across)
    to1 = remote(hid.at[t], hid.at[t], h1_s, h1_r, side1)

    def part_of(block, c):
        return hid.at[block, pl.ds(c * chunk, chunk)]

    to2 = [
        remote(part_of(t, c), part_of(t, c), h2_s.at[c], h2_r.at[c], side2) for c in range(4)
    ]
    from2 = [
        remote(part_of(t2, c), part_of(t2, c), h2_s.at[c], h2_r.at[c], side2) for c in range(4)
    ]
    on1 = [
        remote(part_of(t2, c), part_of(t2, c), hf_s.at[c], hf_r.at[c], side1) for c in range(4)
    ]
    by1 = [
        remote(part_of(t3, c), part_of(t3, c), hf_s.at[c], hf_r.at[c], side1) for c in range(4)
    ]
    x_pos.start()
    send_line(0, 0, 0)
    send_line(0, 1, 0)
    for c in to2:
        c.start()
    x_rows.start()
    to1.start()
    send_line(1, 0, 0)
    send_line(1, 1, 0)

    tile = 256

    def base(block, k, start):
        w_copies[k].wait()
        span = pl.ds(pl.multiple_of(block * width, width), width)

        @pl.loop(0, out_cols // tile)
        def _(n):
            cols = pl.ds(pl.multiple_of(n * tile, tile), tile)
            value = jnp.dot(hid[block], w[span, cols], preferred_element_type=F32)
            if start:
                acc[:, cols] = value
            else:
                acc[:, cols] += value

    half = lax.broadcasted_iota(jnp.int32, (count // 4, 2 * ADAPTER_RANK), 1) // ADAPTER_RANK

    def keep(which, wanted):
        m = jnp.where(wanted, 1, 0)
        return jnp.concatenate([m] * 4, axis=0) > 0

    def shrink(which, slot, start=False):
        source = hid[t] if which == 0 else rows_x[...]
        value = lax.dot_general(
            source, downs[slot], (((1,), (1,)), ((), ())), preferred_element_type=F32
        )
        value = jnp.where(
            keep(which, pos[which] == 2 * (2 * slot + p) + half), value, 0.0
        )
        if start:
            part[which] = value
        else:
            part[which] += value

    x_pos.wait_recv()
    cross(q)
    base(t, 0, True)
    shrink(0, q, True)

    def pass_on(c):
        from2[c].wait_recv()
        on1[c].start()

    def down_step(s):
        for way in (0, 1):

            @pl.when(arrives(way, s))
            def _():
                line_copy(0, way, s, arrived_slot(way, s)).wait_recv()

            if s + 1 < line:
                send_line(0, way, s + 1)

    def down_use(which, s):
        for way in (0, 1):

            @pl.when(arrives(way, s))
            def _():
                shrink(which, arrived_slot(way, s))

    def up_step(s):
        for way in (0, 1):

            @pl.when(arrives(way, s))
            def _():
                slot = arrived_slot(way, s)
                line_copy(1, way, s, slot).wait_recv()
                cross(slot)

            if s + 1 < line:
                send_line(1, way, s + 1)

    pass_on(0)
    pass_on(1)
    down_step(0)
    down_use(0, 0)
    pass_on(2)
    up_step(0)
    pass_on(3)
    to1.wait_recv()
    base(t1, 1, False)
    x_rows.wait_recv()
    shrink(1, q, True)
    down_use(1, 0)
    base(t2, 2, False)
    for s in range(1, line - 1):
        down_step(s)
        down_use(0, s)
        down_use(1, s)
        if s == 1:
            for c in by1:
                c.wait_recv()
            base(t3, 3, False)
        if s < line - 2:
            up_step(s)

    rank = ADAPTER_RANK
    fold = count // 2
    left = lax.broadcasted_iota(jnp.int32, (fold, 2 * rank), 1) < rank

    def pack(value):
        both = value + pltpu.roll(value, rank, 1)
        return jnp.where(left, both[:fold], both[fold:])

    def unpack(value):
        turned = pltpu.roll(value, rank, 1)
        return jnp.concatenate(
            [jnp.where(left, value, turned), jnp.where(left, turned, value)], axis=0
        )

    packed[0] = pack(part[1])
    to_x = remote(packed.at[0], got.at[0], red_s.at[0], red_r.at[0], across)
    to_x.start()
    mine = pack(part[0])
    to_x.wait_recv()
    packed[1] = mine + got[0]
    to_1 = remote(packed.at[1], got.at[1], red_s.at[1], red_r.at[1], side1)
    to_1.start()
    to_1.wait_recv()
    packed[2] = packed[1] + got[1]
    to_2 = remote(packed.at[2], got.at[2], red_s.at[2], red_r.at[2], side2)
    to_2.start()
    up_step(line - 2)
    to_2.wait_recv()
    total = unpack(packed[2] + got[2]).astype(BF16)
    nothing = jnp.zeros_like(total)

    def expand(picked, maps_ref, last):
        @pl.loop(0, out_cols // tile)
        def _(n):
            cols = pl.ds(pl.multiple_of(n * tile, tile), tile)
            maps = maps_ref[:, :, cols].reshape(picked.shape[1], tile)
            value = acc[:, cols] + jnp.dot(picked, maps, preferred_element_type=F32)
            if last:
                query_ref[:, cols] = value.astype(BF16)
            else:
                acc[:, cols] = value

    own = [
        jnp.where(keep(0, pos[0] == 2 * (2 * slot + p) + half), total, nothing)
        for slot in range(line)
    ]
    expand(jnp.concatenate(own, axis=1), ups, False)
    for slot in range(line):
        cross_copy(slot).wait_recv()
    theirs = [
        jnp.where(keep(0, pos[0] // 2 == 2 * (slot + half) + other), total, nothing)
        for slot in range(0, line, 2)
    ]
    expand(jnp.concatenate(theirs, axis=1), ups_x, True)

    x_rows.wait_send()
    x_pos.wait_send()
    to1.wait_send()
    for c in to2 + on1:
        c.wait_send()
    for c in (to_x, to_1, to_2):
        c.wait_send()
    for slot in range(line):
        cross_copy(slot).wait_send()
    for s in range(line):
        for way in (0, 1):

            @pl.when(sends(way, s))
            def _():
                slot = sent_slot(way, s)
                line_copy(0, way, s, slot).wait_send()
                line_copy(1, way, s, slot).wait_send()


def project(token_rows, weight, down, up, position, line):
    count, width = token_rows.shape
    cols = weight.shape[1]
    pages = 2 * ADAPTER_RANK
    anywhere = pl.BlockSpec(memory_space=pl.ANY)
    sems = pltpu.SemaphoreType.DMA
    return pl.pallas_call(
        functools.partial(project_kernel, line),
        out_shape=jax.ShapeDtypeStruct((count, cols), BF16),
        in_specs=[anywhere] * 5,
        out_specs=pl.BlockSpec(memory_space=pltpu.VMEM),
        scratch_shapes=[
            pltpu.VMEM((4, count, width), BF16),
            pltpu.VMEM((count, width), BF16),
            pltpu.VMEM((2, count // 4, pages), jnp.int32),
            pltpu.VMEM((line, pages, width), BF16),
            pltpu.VMEM((line, pages, cols), BF16),
            pltpu.VMEM((line, pages // 2, cols), BF16),
            pltpu.VMEM((line, pages // 2, cols), BF16),
            pltpu.VMEM(weight.shape, BF16),
            pltpu.VMEM((count, cols), F32),
            pltpu.VMEM((2, count, pages), F32),
            pltpu.VMEM((3, count // 2, pages), F32),
            pltpu.VMEM((3, count // 2, pages), F32),
            sems((4,)),
            sems((4,)),
            sems,
            sems,
            sems((4,)),
            sems((4,)),
            sems((4,)),
            sems((4,)),
            sems((2,)),
            sems((2,)),
            sems((2, line)),
            sems((2, line)),
            sems((2, line)),
            sems((2, line)),
            sems((line,)),
            sems((line,)),
            sems((3,)),
            sems((3,)),
        ],
        compiler_params=pltpu.CompilerParams(
            collective_id=0, has_side_effects=True, vmem_limit_bytes=56 * 2**20
        ),
    )(token_rows, weight, down, up, position)


def attend_kernel(steps, q_ref, k_ref, v_ref, nk_ref, nv_ref, len_ref, out_ref):
    q = q_ref[...]
    scale = 1.0 / math.sqrt(HEAD_SIZE)
    dims = (((2,), (2,)), ((0,), (0,)))
    cached = lax.dot_general(q, k_ref[0], dims, preferred_element_type=F32) * scale
    fresh = lax.dot_general(q, nk_ref[...], dims, preferred_element_type=F32) * scale
    place = lax.broadcasted_iota(jnp.int32, cached.shape, 2)
    cached = jnp.where(place < len_ref[...], cached, -1e30)
    step = lax.broadcasted_iota(jnp.int32, fresh.shape, 1) // (q.shape[1] // steps)
    fresh = jnp.where(lax.broadcasted_iota(jnp.int32, fresh.shape, 2) <= step, fresh, -1e30)
    top = jnp.maximum(
        jnp.max(cached, axis=-1, keepdims=True), jnp.max(fresh, axis=-1, keepdims=True)
    )
    cached = jnp.exp(cached - top)
    fresh = jnp.exp(fresh - top)
    total = jnp.sum(cached, axis=-1, keepdims=True) + jnp.sum(fresh, axis=-1, keepdims=True)
    dims = (((2,), (1,)), ((0,), (0,)))
    mixed = lax.dot_general(cached.astype(BF16), v_ref[0], dims, preferred_element_type=F32)
    mixed += lax.dot_general(fresh.astype(BF16), nv_ref[...], dims, preferred_element_type=F32)
    out_ref[...] = (mixed / total).astype(BF16)


def attend(query, cache, fresh, lengths, steps):
    requests, rows, size = query.shape
    length = cache.shape[2]
    pad = fresh.shape[2]
    block = 8

    def spec(which, n):
        return pl.BlockSpec((1, block, n, size), lambda i: (which, i, 0, 0))

    def plain(n):
        return pl.BlockSpec((block, n, size), lambda i: (i, 0, 0))

    return pl.pallas_call(
        functools.partial(attend_kernel, steps),
        grid=(requests // block,),
        out_shape=jax.ShapeDtypeStruct(query.shape, BF16),
        in_specs=[
            plain(rows),
            spec(0, length),
            spec(1, length),
            plain(pad),
            plain(pad),
            plain(1),
        ],
        out_specs=plain(rows),
        compiler_params=pltpu.CompilerParams(vmem_limit_bytes=32 * 2**20),
    )(query, cache, cache, fresh[0], fresh[1], lengths)


def per_device(line, hidden, weight, down, up, cache, step_kv, valid, adapters, pool):
    steps, requests, width = hidden.shape
    table = jnp.arange(pool.shape[0], dtype=jnp.int32)
    position = jnp.sum(jnp.where(adapters[:, None] == table[None, :], pool[None, :], 0), axis=1)
    position = jnp.broadcast_to(position[:, None], (requests, 2 * ADAPTER_RANK))
    query = project(hidden.reshape(steps * requests, width), weight, down, up, position, line)
    heads = weight.shape[1] // HEAD_SIZE
    query = query.reshape(steps, requests, heads, HEAD_SIZE).transpose(1, 0, 2, 3)
    fresh = jnp.pad(step_kv.transpose(1, 2, 0, 3), ((0, 0), (0, 0), (0, 16 - steps), (0, 0)))
    lengths = jnp.broadcast_to(valid[:, None, None], (requests, 1, HEAD_SIZE))
    out = attend(
        query.reshape(requests, steps * heads, HEAD_SIZE), cache, fresh, lengths, steps
    )
    out = out.reshape(requests, steps, heads * HEAD_SIZE)
    return out.transpose(1, 0, 2)


def solution(mesh):
    return jax.shard_map(
        functools.partial(per_device, mesh.shape["dp"] // 2),
        mesh=mesh,
        in_specs=(
            P(None, "dp", "tensor"),
            P(None, "tensor"),
            P("dp", "tensor"),
            P("dp", "tensor"),
            P(None, "dp", None, "tensor"),
            P(None, None, "dp", "tensor"),
            P("dp"),
            P("dp"),
            P(),
        ),
        out_specs=P(None, "dp", "tensor"),
        check_vma=False,
    )
```

```python
import functools
import math

import jax
import jax.numpy as jnp
from jax import lax
from jax.experimental import pallas as pl
from jax.experimental.pallas import tpu as pltpu
from jax.sharding import PartitionSpec as P

HEAD_SIZE = 128
ADAPTER_RANK = 64
MESH = pl.DeviceIdType.MESH
F32 = jnp.float32
BF16 = jnp.bfloat16


def project_kernel(
    line,
    hid_hbm,
    w_hbm,
    down_hbm,
    up_hbm,
    pos_hbm,
    query_ref,
    hid,
    rows_x,
    pos,
    downs,
    ups,
    picks,
    ups_x,
    w,
    acc,
    part,
    packed,
    got,
    local_sem,
    w_sem,
    h1_s,
    h1_r,
    h2_s,
    h2_r,
    hf_s,
    hf_r,
    x_s,
    x_r,
    zd_s,
    zd_r,
    zu_s,
    zu_r,
    xu_s,
    xu_r,
    red_s,
    red_r,
    far,
    far_pos,
    far_part,
    far_pack,
    far_got,
    far_s,
    far_r,
):
    d = lax.axis_index("dp")
    t = lax.axis_index("tensor")
    q, p = d // 2, d % 2
    other = 1 - p
    t1 = t + 1 - 2 * (t % 2)
    t2 = (t + 2) % 4
    t3 = (t1 + 2) % 4
    above, below, across = (d + 2, t), (d - 2, t), (d + 1 - 2 * p, t)
    side1, side2 = (d, t1), (d, t2)
    count = hid.shape[1]
    width = hid.shape[2]
    chunk = count // 4
    out_cols = w.shape[1]
    has_above, has_below = q < line - 1, q > 0
    near = width - far.shape[2]
    is_end = jnp.logical_or(q == 0, q == line - 1)
    is_next = jnp.logical_or(q == 1, q == line - 2)
    inner = (jnp.where(q == 0, d + 2, d - 2), t)
    outer = (jnp.where(q == 1, d - 2, d + 2), t)

    def local(src, dst, k):
        return pltpu.make_async_copy(src, dst, local_sem.at[k])

    def remote(src, dst, s, r, to):
        return pltpu.make_async_remote_copy(
            src_ref=src, dst_ref=dst, send_sem=s, recv_sem=r, device_id=to, device_id_type=MESH
        )

    first = [
        local(down_hbm, downs.at[q], 0),
        local(hid_hbm, hid.at[t], 1),
        local(pos_hbm, pos.at[0], 2),
        local(up_hbm, ups.at[q], 3),
    ]
    for c in first:
        c.start()
    order = [t, t1, t2, t3]
    w_copies = []
    for k, block in enumerate(order):
        span = pl.ds(pl.multiple_of(block * width, width), width)
        w_copies.append(pltpu.make_async_copy(w_hbm.at[span], w.at[span], w_sem.at[k]))
        w_copies[-1].start()

    barrier = pltpu.get_barrier_semaphore()
    for peer in (across, side1, side2):
        pl.semaphore_signal(barrier, inc=1, device_id=peer, device_id_type=MESH)

    @pl.when(has_above)
    def _():
        pl.semaphore_signal(barrier, inc=1, device_id=above, device_id_type=MESH)

    @pl.when(has_below)
    def _():
        pl.semaphore_signal(barrier, inc=1, device_id=below, device_id_type=MESH)

    pl.semaphore_wait(
        barrier, 3 + jnp.where(has_above, 1, 0) + jnp.where(has_below, 1, 0)
    )
    for c in first:
        c.wait()

    def line_copy(kind, way, s, slot, short=False):
        ref = downs.at[slot] if kind == 0 else ups.at[slot]
        if short:
            ref = downs.at[slot, :, pl.ds(0, near)]
        send, recv = (zd_s, zd_r) if kind == 0 else (zu_s, zu_r)
        return remote(
            ref, ref, send.at[way, s], recv.at[way, s], above if way == 0 else below
        )

    def to_end(way):
        return q == line - 2 if way == 0 else q == 1

    def both(kind, cond, short, act):
        if kind == 1:
            pl.when(cond)(lambda: act(False))
        else:
            pl.when(jnp.logical_and(cond, short))(lambda: act(True))
            pl.when(jnp.logical_and(cond, jnp.logical_not(short)))(lambda: act(False))

    def sends(way, s):
        if way == 0:
            return jnp.logical_and(has_above, q - s >= 0)
        return jnp.logical_and(has_below, q + s <= line - 1)

    def sent_slot(way, s):
        return q - s if way == 0 else q + s

    def arrives(way, s):
        return q - 1 - s >= 0 if way == 0 else q + 1 + s <= line - 1

    def arrived_slot(way, s):
        return q - 1 - s if way == 0 else q + 1 + s

    def send_line(kind, way, s):
        both(
            kind,
            sends(way, s),
            to_end(way),
            lambda short: line_copy(kind, way, s, sent_slot(way, s), short).start(),
        )

    def cross_copy(slot):
        return remote(picks.at[slot], ups_x.at[slot], xu_s.at[slot], xu_r.at[slot], across)

    def cross(slot):
        second = jnp.where(pos[1] == 2 * (2 * slot + p) + 1, 1.0, 0.0)
        second = jnp.max(second, axis=0, keepdims=True)
        second = jnp.broadcast_to(second, (ADAPTER_RANK, second.shape[1])) > 0.5
        for c in range(0, out_cols, 2 * ADAPTER_RANK):
            cols = pl.ds(c, 2 * ADAPTER_RANK)
            picks[slot, :, cols] = jnp.where(
                second,
                ups[slot, pl.ds(ADAPTER_RANK, ADAPTER_RANK), cols],
                ups[slot, pl.ds(0, ADAPTER_RANK), cols],
            )
        cross_copy(slot).start()

    x_rows = remote(hid.at[t], rows_x, x_s.at[0], x_r.at[0], across)
    x_pos = remote(pos.at[0], pos.at[1], x_s.at[1], x_r.at[1], across)
    to1 = remote(hid.at[t], hid.at[t], h1_s, h1_r, side1)

    def part_of(block, c):
        return hid.at[block, pl.ds(c * chunk, chunk)]

    to2 = [
        remote(part_of(t, c), part_of(t, c), h2_s.at[c], h2_r.at[c], side2) for c in range(4)
    ]
    from2 = [
        remote(part_of(t2, c), part_of(t2, c), h2_s.at[c], h2_r.at[c], side2) for c in range(4)
    ]
    on1 = [
        remote(part_of(t2, c), part_of(t2, c), hf_s.at[c], hf_r.at[c], side1) for c in range(4)
    ]
    by1 = [
        remote(part_of(t3, c), part_of(t3, c), hf_s.at[c], hf_r.at[c], side1) for c in range(4)
    ]
    x_pos.start()
    send_line(0, 0, 0)
    send_line(0, 1, 0)
    for c in to2:
        c.start()
    x_rows.start()
    to1.start()
    rest = pl.ds(near, width - near)
    far_rows = [
        remote(src, far.at[g], far_s.at[g], far_r.at[g], inner)
        for g, src in enumerate((hid.at[t, :, rest], rows_x.at[:, rest]))
    ]
    far_places = [
        remote(pos.at[g], far_pos.at[g], far_s.at[2 + g], far_r.at[2 + g], inner)
        for g in (0, 1)
    ]
    far_back = [
        remote(far_pack.at[g], far_got.at[g], far_s.at[4 + g], far_r.at[4 + g], outer)
        for g in (0, 1)
    ]

    @pl.when(is_end)
    def _():
        far_places[0].start()
        far_rows[0].start()

    send_line(1, 0, 0)
    send_line(1, 1, 0)

    tile = 256

    def base(block, k, start):
        w_copies[k].wait()
        span = pl.ds(pl.multiple_of(block * width, width), width)

        @pl.loop(0, out_cols // tile)
        def _(n):
            cols = pl.ds(pl.multiple_of(n * tile, tile), tile)
            value = jnp.dot(hid[block], w[span, cols], preferred_element_type=F32)
            if start:
                acc[:, cols] = value
            else:
                acc[:, cols] += value

    half = lax.broadcasted_iota(jnp.int32, (count // 4, 2 * ADAPTER_RANK), 1) // ADAPTER_RANK

    def keep(which, wanted):
        m = jnp.where(wanted, 1, 0)
        return jnp.concatenate([m] * 4, axis=0) > 0

    def shrink(which, slot, start=False, short=False):
        cols = pl.ds(0, near if short else width)
        source = hid[t, :, cols] if which == 0 else rows_x[:, cols]
        value = lax.dot_general(
            source, downs[slot, :, cols], (((1,), (1,)), ((), ())), preferred_element_type=F32
        )
        value = jnp.where(
            keep(which, pos[which] == 2 * (2 * slot + p) + half), value, 0.0
        )
        if start:
            part[which] = value
        else:
            part[which] += value

    x_pos.wait_recv()
    cross(q)
    base(t, 0, True)
    shrink(0, q, True)

    def pass_on(c):
        from2[c].wait_recv()
        on1[c].start()

    def down_step(s):
        for way in (0, 1):

            both(
                0,
                arrives(way, s),
                is_end,
                lambda short: line_copy(0, way, s, arrived_slot(way, s), short).wait_recv(),
            )

            if s + 1 < line:
                send_line(0, way, s + 1)

    def down_use(which, s):
        for way in (0, 1):

            both(
                0,
                arrives(way, s),
                is_end,
                lambda short: shrink(which, arrived_slot(way, s), False, short),
            )

    def up_step(s):
        for way in (0, 1):

            @pl.when(arrives(way, s))
            def _():
                slot = arrived_slot(way, s)
                line_copy(1, way, s, slot).wait_recv()
                cross(slot)

            if s + 1 < line:
                send_line(1, way, s + 1)

    rank = ADAPTER_RANK
    fold = count // 2
    left = lax.broadcasted_iota(jnp.int32, (fold, 2 * rank), 1) < rank

    def pack(value):
        both = value + pltpu.roll(value, rank, 1)
        return jnp.where(left, both[:fold], both[fold:])

    def unpack(value):
        turned = pltpu.roll(value, rank, 1)
        return jnp.concatenate(
            [jnp.where(left, value, turned), jnp.where(left, turned, value)], axis=0
        )

    def far_use():
        for g in (0, 1):
            far_places[g].wait_recv()
            far_rows[g].wait_recv()
            far_part[...] = jnp.zeros_like(far_part)

            @pl.loop(0, line - 1)
            def _(i):
                slot = i + jnp.where(q == 1, 1, 0)
                value = lax.dot_general(
                    far[g],
                    downs[slot, :, rest],
                    (((1,), (1,)), ((), ())),
                    preferred_element_type=F32,
                )
                wanted = far_pos[g] == 2 * (2 * slot + p) + half
                far_part[...] += jnp.where(keep(g, wanted), value, 0.0)

            far_pack[g] = pack(far_part[...])
            far_back[g].start()

    pass_on(0)
    pass_on(1)
    down_step(0)
    down_use(0, 0)
    pass_on(2)
    up_step(0)
    pass_on(3)
    to1.wait_recv()
    base(t1, 1, False)
    x_rows.wait_recv()

    @pl.when(is_end)
    def _():
        far_places[1].start()
        far_rows[1].start()

    shrink(1, q, True)
    down_use(1, 0)
    base(t2, 2, False)
    for s in range(1, line - 1):
        down_step(s)
        down_use(0, s)
        down_use(1, s)
        if s == 1:
            for c in by1:
                c.wait_recv()
            base(t3, 3, False)
        if s < line - 2:
            up_step(s)
        if s == line - 3:
            pl.when(is_next)(far_use)

    @pl.when(is_end)
    def _():
        for g in (0, 1):
            far_back[g].wait_recv()
            part[g] += jnp.where(keep(g, pos[g] % 2 == half), unpack(far_got[g]), 0.0)

    packed[0] = pack(part[1])
    to_x = remote(packed.at[0], got.at[0], red_s.at[0], red_r.at[0], across)
    to_x.start()
    mine = pack(part[0])
    to_x.wait_recv()
    packed[1] = mine + got[0]
    to_1 = remote(packed.at[1], got.at[1], red_s.at[1], red_r.at[1], side1)
    to_1.start()
    to_1.wait_recv()
    packed[2] = packed[1] + got[1]
    to_2 = remote(packed.at[2], got.at[2], red_s.at[2], red_r.at[2], side2)
    to_2.start()
    up_step(line - 2)
    to_2.wait_recv()
    total = unpack(packed[2] + got[2]).astype(BF16)
    nothing = jnp.zeros_like(total)

    def expand(picked, maps_ref, last):
        @pl.loop(0, out_cols // tile)
        def _(n):
            cols = pl.ds(pl.multiple_of(n * tile, tile), tile)
            maps = maps_ref[:, :, cols].reshape(picked.shape[1], tile)
            value = acc[:, cols] + jnp.dot(picked, maps, preferred_element_type=F32)
            if last:
                query_ref[:, cols] = value.astype(BF16)
            else:
                acc[:, cols] = value

    own = [
        jnp.where(keep(0, pos[0] == 2 * (2 * slot + p) + half), total, nothing)
        for slot in range(line)
    ]
    expand(jnp.concatenate(own, axis=1), ups, False)
    for slot in range(line):
        cross_copy(slot).wait_recv()
    theirs = [
        jnp.where(keep(0, pos[0] // 2 == 2 * (slot + half) + other), total, nothing)
        for slot in range(0, line, 2)
    ]
    expand(jnp.concatenate(theirs, axis=1), ups_x, True)

    x_rows.wait_send()
    x_pos.wait_send()
    to1.wait_send()
    for c in to2 + on1:
        c.wait_send()
    for c in (to_x, to_1, to_2):
        c.wait_send()
    for slot in range(line):
        cross_copy(slot).wait_send()
    @pl.when(is_end)
    def _():
        for c in far_places + far_rows:
            c.wait_send()

    @pl.when(is_next)
    def _():
        for c in far_back:
            c.wait_send()

    for s in range(line):
        for way in (0, 1):
            for kind in (0, 1):
                both(
                    kind,
                    sends(way, s),
                    to_end(way),
                    lambda short: line_copy(kind, way, s, sent_slot(way, s), short).wait_send(),
                )


def project(token_rows, weight, down, up, position, line):
    count, width = token_rows.shape
    cols = weight.shape[1]
    pages = 2 * ADAPTER_RANK
    anywhere = pl.BlockSpec(memory_space=pl.ANY)
    sems = pltpu.SemaphoreType.DMA
    return pl.pallas_call(
        functools.partial(project_kernel, line),
        out_shape=jax.ShapeDtypeStruct((count, cols), BF16),
        in_specs=[anywhere] * 5,
        out_specs=pl.BlockSpec(memory_space=pltpu.VMEM),
        scratch_shapes=[
            pltpu.VMEM((4, count, width), BF16),
            pltpu.VMEM((count, width), BF16),
            pltpu.VMEM((2, count // 4, pages), jnp.int32),
            pltpu.VMEM((line, pages, width), BF16),
            pltpu.VMEM((line, pages, cols), BF16),
            pltpu.VMEM((line, pages // 2, cols), BF16),
            pltpu.VMEM((line, pages // 2, cols), BF16),
            pltpu.VMEM(weight.shape, BF16),
            pltpu.VMEM((count, cols), F32),
            pltpu.VMEM((2, count, pages), F32),
            pltpu.VMEM((3, count // 2, pages), F32),
            pltpu.VMEM((3, count // 2, pages), F32),
            sems((4,)),
            sems((4,)),
            sems,
            sems,
            sems((4,)),
            sems((4,)),
            sems((4,)),
            sems((4,)),
            sems((2,)),
            sems((2,)),
            sems((2, line)),
            sems((2, line)),
            sems((2, line)),
            sems((2, line)),
            sems((line,)),
            sems((line,)),
            sems((3,)),
            sems((3,)),
            pltpu.VMEM((2, count, width * 3 // 8), BF16),
            pltpu.VMEM((2, count // 4, pages), jnp.int32),
            pltpu.VMEM((count, pages), F32),
            pltpu.VMEM((2, count // 2, pages), F32),
            pltpu.VMEM((2, count // 2, pages), F32),
            sems((6,)),
            sems((6,)),
        ],
        compiler_params=pltpu.CompilerParams(
            collective_id=0, has_side_effects=True, vmem_limit_bytes=56 * 2**20
        ),
    )(token_rows, weight, down, up, position)


def attend_kernel(steps, q_ref, k_ref, v_ref, nk_ref, nv_ref, len_ref, out_ref):
    q = q_ref[...]
    scale = 1.0 / math.sqrt(HEAD_SIZE)
    dims = (((2,), (2,)), ((0,), (0,)))
    cached = lax.dot_general(q, k_ref[0], dims, preferred_element_type=F32) * scale
    fresh = lax.dot_general(q, nk_ref[...], dims, preferred_element_type=F32) * scale
    place = lax.broadcasted_iota(jnp.int32, cached.shape, 2)
    cached = jnp.where(place < len_ref[...], cached, -1e30)
    step = lax.broadcasted_iota(jnp.int32, fresh.shape, 1) // (q.shape[1] // steps)
    fresh = jnp.where(lax.broadcasted_iota(jnp.int32, fresh.shape, 2) <= step, fresh, -1e30)
    top = jnp.maximum(
        jnp.max(cached, axis=-1, keepdims=True), jnp.max(fresh, axis=-1, keepdims=True)
    )
    cached = jnp.exp(cached - top)
    fresh = jnp.exp(fresh - top)
    total = jnp.sum(cached, axis=-1, keepdims=True) + jnp.sum(fresh, axis=-1, keepdims=True)
    dims = (((2,), (1,)), ((0,), (0,)))
    mixed = lax.dot_general(cached.astype(BF16), v_ref[0], dims, preferred_element_type=F32)
    mixed += lax.dot_general(fresh.astype(BF16), nv_ref[...], dims, preferred_element_type=F32)
    out_ref[...] = (mixed / total).astype(BF16)


def attend(query, cache, fresh, lengths, steps):
    requests, rows, size = query.shape
    length = cache.shape[2]
    pad = fresh.shape[2]
    block = 8

    def spec(which, n):
        return pl.BlockSpec((1, block, n, size), lambda i: (which, i, 0, 0))

    def plain(n):
        return pl.BlockSpec((block, n, size), lambda i: (i, 0, 0))

    return pl.pallas_call(
        functools.partial(attend_kernel, steps),
        grid=(requests // block,),
        out_shape=jax.ShapeDtypeStruct(query.shape, BF16),
        in_specs=[
            plain(rows),
            spec(0, length),
            spec(1, length),
            plain(pad),
            plain(pad),
            plain(1),
        ],
        out_specs=plain(rows),
        compiler_params=pltpu.CompilerParams(vmem_limit_bytes=32 * 2**20),
    )(query, cache, cache, fresh[0], fresh[1], lengths)


def per_device(line, hidden, weight, down, up, cache, step_kv, valid, adapters, pool):
    steps, requests, width = hidden.shape
    table = jnp.arange(pool.shape[0], dtype=jnp.int32)
    position = jnp.sum(jnp.where(adapters[:, None] == table[None, :], pool[None, :], 0), axis=1)
    position = jnp.broadcast_to(position[:, None], (requests, 2 * ADAPTER_RANK))
    query = project(hidden.reshape(steps * requests, width), weight, down, up, position, line)
    heads = weight.shape[1] // HEAD_SIZE
    query = query.reshape(steps, requests, heads, HEAD_SIZE).transpose(1, 0, 2, 3)
    fresh = jnp.pad(step_kv.transpose(1, 2, 0, 3), ((0, 0), (0, 0), (0, 16 - steps), (0, 0)))
    lengths = jnp.broadcast_to(valid[:, None, None], (requests, 1, HEAD_SIZE))
    out = attend(
        query.reshape(requests, steps * heads, HEAD_SIZE), cache, fresh, lengths, steps
    )
    out = out.reshape(requests, steps, heads * HEAD_SIZE)
    return out.transpose(1, 0, 2)


def solution(mesh):
    return jax.shard_map(
        functools.partial(per_device, mesh.shape["dp"] // 2),
        mesh=mesh,
        in_specs=(
            P(None, "dp", "tensor"),
            P(None, "tensor"),
            P("dp", "tensor"),
            P("dp", "tensor"),
            P(None, "dp", None, "tensor"),
            P(None, None, "dp", "tensor"),
            P("dp"),
            P("dp"),
            P(),
        ),
        out_specs=P(None, "dp", "tensor"),
        check_vma=False,
    )
```

```python
import functools
import math

import jax
import jax.numpy as jnp
from jax import lax
from jax.experimental import pallas as pl
from jax.experimental.pallas import tpu as pltpu
from jax.sharding import PartitionSpec as P

HEAD_SIZE = 128
ADAPTER_RANK = 64
MESH = pl.DeviceIdType.MESH
F32 = jnp.float32
BF16 = jnp.bfloat16


def project_kernel(
    line,
    hid_hbm,
    w_hbm,
    down_hbm,
    up_hbm,
    pos_hbm,
    query_ref,
    hid,
    rows_x,
    pos,
    downs,
    ups,
    picks,
    ups_x,
    w,
    acc,
    part,
    packed,
    got,
    local_sem,
    w_sem,
    h1_s,
    h1_r,
    h2_s,
    h2_r,
    hf_s,
    hf_r,
    x_s,
    x_r,
    zd_s,
    zd_r,
    zu_s,
    zu_r,
    xu_s,
    xu_r,
    red_s,
    red_r,
    far,
    far_pos,
    far_part,
    far_pack,
    far_got,
    far_s,
    far_r,
):
    d = lax.axis_index("dp")
    t = lax.axis_index("tensor")
    q, p = d // 2, d % 2
    other = 1 - p
    t1 = t + 1 - 2 * (t % 2)
    t2 = (t + 2) % 4
    t3 = (t1 + 2) % 4
    above, below, across = (d + 2, t), (d - 2, t), (d + 1 - 2 * p, t)
    side1, side2 = (d, t1), (d, t2)
    count = hid.shape[1]
    width = hid.shape[2]
    chunk = count // 4
    out_cols = w.shape[1]
    has_above, has_below = q < line - 1, q > 0
    near = width - far.shape[2]
    is_end = jnp.logical_or(q == 0, q == line - 1)
    is_next = jnp.logical_or(q == 1, q == line - 2)
    inner = (jnp.where(q == 0, d + 2, d - 2), t)
    outer = (jnp.where(q == 1, d - 2, d + 2), t)

    def local(src, dst, k):
        return pltpu.make_async_copy(src, dst, local_sem.at[k])

    def remote(src, dst, s, r, to):
        return pltpu.make_async_remote_copy(
            src_ref=src, dst_ref=dst, send_sem=s, recv_sem=r, device_id=to, device_id_type=MESH
        )

    first = [
        local(down_hbm, downs.at[q], 0),
        local(hid_hbm, hid.at[t], 1),
        local(pos_hbm, pos.at[0], 2),
        local(up_hbm, ups.at[q], 3),
    ]
    for c in first:
        c.start()
    order = [t, t1, t2, t3]
    w_copies = []
    for k, block in enumerate(order):
        span = pl.ds(pl.multiple_of(block * width, width), width)
        w_copies.append(pltpu.make_async_copy(w_hbm.at[span], w.at[span], w_sem.at[k]))
        w_copies[-1].start()

    barrier = pltpu.get_barrier_semaphore()
    for peer in (across, side1, side2):
        pl.semaphore_signal(barrier, inc=1, device_id=peer, device_id_type=MESH)

    @pl.when(has_above)
    def _():
        pl.semaphore_signal(barrier, inc=1, device_id=above, device_id_type=MESH)

    @pl.when(has_below)
    def _():
        pl.semaphore_signal(barrier, inc=1, device_id=below, device_id_type=MESH)

    pl.semaphore_wait(
        barrier, 3 + jnp.where(has_above, 1, 0) + jnp.where(has_below, 1, 0)
    )
    for c in first:
        c.wait()

    def line_copy(kind, way, s, slot, short=False):
        ref = downs.at[slot] if kind == 0 else ups.at[slot]
        if short:
            ref = downs.at[slot, :, pl.ds(0, near)]
        send, recv = (zd_s, zd_r) if kind == 0 else (zu_s, zu_r)
        return remote(
            ref, ref, send.at[way, s], recv.at[way, s], above if way == 0 else below
        )

    def to_end(way):
        return q == line - 2 if way == 0 else q == 1

    def both(kind, cond, short, act):
        if kind == 1:
            pl.when(cond)(lambda: act(False))
        else:
            pl.when(jnp.logical_and(cond, short))(lambda: act(True))
            pl.when(jnp.logical_and(cond, jnp.logical_not(short)))(lambda: act(False))

    def sends(way, s):
        if way == 0:
            return jnp.logical_and(has_above, q - s >= 0)
        return jnp.logical_and(has_below, q + s <= line - 1)

    def sent_slot(way, s):
        return q - s if way == 0 else q + s

    def arrives(way, s):
        return q - 1 - s >= 0 if way == 0 else q + 1 + s <= line - 1

    def arrived_slot(way, s):
        return q - 1 - s if way == 0 else q + 1 + s

    def send_line(kind, way, s):
        both(
            kind,
            sends(way, s),
            to_end(way),
            lambda short: line_copy(kind, way, s, sent_slot(way, s), short).start(),
        )

    def cross_copy(slot):
        return remote(picks.at[slot], ups_x.at[slot], xu_s.at[slot], xu_r.at[slot], across)

    def cross(slot):
        second = jnp.where(pos[1] == 2 * (2 * slot + p) + 1, 1.0, 0.0)
        second = jnp.max(second, axis=0, keepdims=True)
        second = jnp.broadcast_to(second, (ADAPTER_RANK, second.shape[1])) > 0.5
        for c in range(0, out_cols, 2 * ADAPTER_RANK):
            cols = pl.ds(c, 2 * ADAPTER_RANK)
            picks[slot, :, cols] = jnp.where(
                second,
                ups[slot, pl.ds(ADAPTER_RANK, ADAPTER_RANK), cols],
                ups[slot, pl.ds(0, ADAPTER_RANK), cols],
            )
        cross_copy(slot).start()

    x_rows = remote(hid.at[t], rows_x, x_s.at[0], x_r.at[0], across)
    x_pos = remote(pos.at[0], pos.at[1], x_s.at[1], x_r.at[1], across)
    to1 = remote(hid.at[t], hid.at[t], h1_s, h1_r, side1)

    def part_of(block, c):
        return hid.at[block, pl.ds(c * chunk, chunk)]

    to2 = [
        remote(part_of(t, c), part_of(t, c), h2_s.at[c], h2_r.at[c], side2) for c in range(4)
    ]
    from2 = [
        remote(part_of(t2, c), part_of(t2, c), h2_s.at[c], h2_r.at[c], side2) for c in range(4)
    ]
    on1 = [
        remote(part_of(t2, c), part_of(t2, c), hf_s.at[c], hf_r.at[c], side1) for c in range(4)
    ]
    by1 = [
        remote(part_of(t3, c), part_of(t3, c), hf_s.at[c], hf_r.at[c], side1) for c in range(4)
    ]
    x_pos.start()
    send_line(0, 0, 0)
    send_line(0, 1, 0)
    for c in to2:
        c.start()
    x_rows.start()
    to1.start()
    rest = pl.ds(near, width - near)
    far_rows = [
        remote(src, far.at[g], far_s.at[g], far_r.at[g], inner)
        for g, src in enumerate((hid.at[t, :, rest], rows_x.at[:, rest]))
    ]
    far_places = [
        remote(pos.at[g], far_pos.at[g], far_s.at[2 + g], far_r.at[2 + g], inner)
        for g in (0, 1)
    ]
    far_back = [
        remote(far_pack.at[g], far_got.at[g], far_s.at[4 + g], far_r.at[4 + g], outer)
        for g in (0, 1)
    ]

    send_line(1, 0, 0)
    send_line(1, 1, 0)

    @pl.when(is_end)
    def _():
        far_places[0].start()
        far_rows[0].start()


    tile = 256

    def base(block, k, start):
        w_copies[k].wait()
        span = pl.ds(pl.multiple_of(block * width, width), width)

        @pl.loop(0, out_cols // tile)
        def _(n):
            cols = pl.ds(pl.multiple_of(n * tile, tile), tile)
            value = jnp.dot(hid[block], w[span, cols], preferred_element_type=F32)
            if start:
                acc[:, cols] = value
            else:
                acc[:, cols] += value

    half = lax.broadcasted_iota(jnp.int32, (count // 4, 2 * ADAPTER_RANK), 1) // ADAPTER_RANK

    def keep(which, wanted):
        m = jnp.where(wanted, 1, 0)
        return jnp.concatenate([m] * 4, axis=0) > 0

    def shrink(which, slot, start=False, short=False):
        cols = pl.ds(0, near if short else width)
        source = hid[t, :, cols] if which == 0 else rows_x[:, cols]
        value = lax.dot_general(
            source, downs[slot, :, cols], (((1,), (1,)), ((), ())), preferred_element_type=F32
        )
        value = jnp.where(
            keep(which, pos[which] == 2 * (2 * slot + p) + half), value, 0.0
        )
        if start:
            part[which] = value
        else:
            part[which] += value

    x_pos.wait_recv()
    cross(q)
    base(t, 0, True)
    shrink(0, q, True)

    def pass_on(c):
        from2[c].wait_recv()
        on1[c].start()

    def down_step(s):
        for way in (0, 1):

            both(
                0,
                arrives(way, s),
                is_end,
                lambda short: line_copy(0, way, s, arrived_slot(way, s), short).wait_recv(),
            )

            if s + 1 < line:
                send_line(0, way, s + 1)

    def down_use(which, s):
        for way in (0, 1):

            both(
                0,
                arrives(way, s),
                is_end,
                lambda short: shrink(which, arrived_slot(way, s), False, short),
            )

    def up_step(s):
        for way in (0, 1):

            @pl.when(arrives(way, s))
            def _():
                slot = arrived_slot(way, s)
                line_copy(1, way, s, slot).wait_recv()
                cross(slot)

            if s + 1 < line:
                send_line(1, way, s + 1)

    rank = ADAPTER_RANK
    fold = count // 2
    left = lax.broadcasted_iota(jnp.int32, (fold, 2 * rank), 1) < rank

    def pack(value):
        both = value + pltpu.roll(value, rank, 1)
        return jnp.where(left, both[:fold], both[fold:])

    def unpack(value):
        turned = pltpu.roll(value, rank, 1)
        return jnp.concatenate(
            [jnp.where(left, value, turned), jnp.where(left, turned, value)], axis=0
        )

    def far_use():
        for g in (0, 1):
            far_places[g].wait_recv()
            far_rows[g].wait_recv()
            far_part[...] = jnp.zeros_like(far_part)

            @pl.loop(0, line - 1)
            def _(i):
                slot = i + jnp.where(q == 1, 1, 0)
                value = lax.dot_general(
                    far[g],
                    downs[slot, :, rest],
                    (((1,), (1,)), ((), ())),
                    preferred_element_type=F32,
                )
                wanted = far_pos[g] == 2 * (2 * slot + p) + half
                far_part[...] += jnp.where(keep(g, wanted), value, 0.0)

            far_pack[g] = pack(far_part[...])
            far_back[g].start()

    pass_on(0)
    pass_on(1)
    down_step(0)
    down_use(0, 0)
    pass_on(2)
    up_step(0)
    pass_on(3)
    to1.wait_recv()
    base(t1, 1, False)
    x_rows.wait_recv()

    @pl.when(is_end)
    def _():
        far_places[1].start()
        far_rows[1].start()

    shrink(1, q, True)
    down_use(1, 0)
    base(t2, 2, False)
    for s in range(1, line - 1):
        down_step(s)
        down_use(0, s)
        down_use(1, s)
        if s == 1:
            for c in by1:
                c.wait_recv()
            base(t3, 3, False)
        if s < line - 2:
            up_step(s)
        if s == line - 3:
            pl.when(is_next)(far_use)

    @pl.when(is_end)
    def _():
        for g in (0, 1):
            far_back[g].wait_recv()
            part[g] += jnp.where(keep(g, pos[g] % 2 == half), unpack(far_got[g]), 0.0)

    packed[0] = pack(part[1])
    to_x = remote(packed.at[0], got.at[0], red_s.at[0], red_r.at[0], across)
    to_x.start()
    mine = pack(part[0])
    to_x.wait_recv()
    packed[1] = mine + got[0]
    to_1 = remote(packed.at[1], got.at[1], red_s.at[1], red_r.at[1], side1)
    to_1.start()
    to_1.wait_recv()
    packed[2] = packed[1] + got[1]
    to_2 = remote(packed.at[2], got.at[2], red_s.at[2], red_r.at[2], side2)
    to_2.start()
    up_step(line - 2)
    to_2.wait_recv()
    total = unpack(packed[2] + got[2]).astype(BF16)
    nothing = jnp.zeros_like(total)

    def expand(picked, maps_ref, last):
        @pl.loop(0, out_cols // tile)
        def _(n):
            cols = pl.ds(pl.multiple_of(n * tile, tile), tile)
            maps = maps_ref[:, :, cols].reshape(picked.shape[1], tile)
            value = acc[:, cols] + jnp.dot(picked, maps, preferred_element_type=F32)
            if last:
                query_ref[:, cols] = value.astype(BF16)
            else:
                acc[:, cols] = value

    own = [
        jnp.where(keep(0, pos[0] == 2 * (2 * slot + p) + half), total, nothing)
        for slot in range(line)
    ]
    expand(jnp.concatenate(own, axis=1), ups, False)
    for slot in range(line):
        cross_copy(slot).wait_recv()
    theirs = [
        jnp.where(keep(0, pos[0] // 2 == 2 * (slot + half) + other), total, nothing)
        for slot in range(0, line, 2)
    ]
    expand(jnp.concatenate(theirs, axis=1), ups_x, True)

    x_rows.wait_send()
    x_pos.wait_send()
    to1.wait_send()
    for c in to2 + on1:
        c.wait_send()
    for c in (to_x, to_1, to_2):
        c.wait_send()
    for slot in range(line):
        cross_copy(slot).wait_send()
    @pl.when(is_end)
    def _():
        for c in far_places + far_rows:
            c.wait_send()

    @pl.when(is_next)
    def _():
        for c in far_back:
            c.wait_send()

    for s in range(line):
        for way in (0, 1):
            for kind in (0, 1):
                both(
                    kind,
                    sends(way, s),
                    to_end(way),
                    lambda short: line_copy(kind, way, s, sent_slot(way, s), short).wait_send(),
                )


def project(token_rows, weight, down, up, position, line):
    count, width = token_rows.shape
    cols = weight.shape[1]
    pages = 2 * ADAPTER_RANK
    anywhere = pl.BlockSpec(memory_space=pl.ANY)
    sems = pltpu.SemaphoreType.DMA
    return pl.pallas_call(
        functools.partial(project_kernel, line),
        out_shape=jax.ShapeDtypeStruct((count, cols), BF16),
        in_specs=[anywhere] * 5,
        out_specs=pl.BlockSpec(memory_space=pltpu.VMEM),
        scratch_shapes=[
            pltpu.VMEM((4, count, width), BF16),
            pltpu.VMEM((count, width), BF16),
            pltpu.VMEM((2, count // 4, pages), jnp.int32),
            pltpu.VMEM((line, pages, width), BF16),
            pltpu.VMEM((line, pages, cols), BF16),
            pltpu.VMEM((line, pages // 2, cols), BF16),
            pltpu.VMEM((line, pages // 2, cols), BF16),
            pltpu.VMEM(weight.shape, BF16),
            pltpu.VMEM((count, cols), F32),
            pltpu.VMEM((2, count, pages), F32),
            pltpu.VMEM((3, count // 2, pages), F32),
            pltpu.VMEM((3, count // 2, pages), F32),
            sems((4,)),
            sems((4,)),
            sems,
            sems,
            sems((4,)),
            sems((4,)),
            sems((4,)),
            sems((4,)),
            sems((2,)),
            sems((2,)),
            sems((2, line)),
            sems((2, line)),
            sems((2, line)),
            sems((2, line)),
            sems((line,)),
            sems((line,)),
            sems((3,)),
            sems((3,)),
            pltpu.VMEM((2, count, width * 3 // 8), BF16),
            pltpu.VMEM((2, count // 4, pages), jnp.int32),
            pltpu.VMEM((count, pages), F32),
            pltpu.VMEM((2, count // 2, pages), F32),
            pltpu.VMEM((2, count // 2, pages), F32),
            sems((6,)),
            sems((6,)),
        ],
        compiler_params=pltpu.CompilerParams(
            collective_id=0, has_side_effects=True, vmem_limit_bytes=56 * 2**20
        ),
    )(token_rows, weight, down, up, position)


def attend_kernel(steps, q_ref, k_ref, v_ref, nk_ref, nv_ref, len_ref, out_ref):
    q = q_ref[...]
    scale = 1.0 / math.sqrt(HEAD_SIZE)
    dims = (((2,), (2,)), ((0,), (0,)))
    cached = lax.dot_general(q, k_ref[0], dims, preferred_element_type=F32) * scale
    fresh = lax.dot_general(q, nk_ref[...], dims, preferred_element_type=F32) * scale
    place = lax.broadcasted_iota(jnp.int32, cached.shape, 2)
    cached = jnp.where(place < len_ref[...], cached, -1e30)
    step = lax.broadcasted_iota(jnp.int32, fresh.shape, 1) // (q.shape[1] // steps)
    fresh = jnp.where(lax.broadcasted_iota(jnp.int32, fresh.shape, 2) <= step, fresh, -1e30)
    top = jnp.maximum(
        jnp.max(cached, axis=-1, keepdims=True), jnp.max(fresh, axis=-1, keepdims=True)
    )
    cached = jnp.exp(cached - top)
    fresh = jnp.exp(fresh - top)
    total = jnp.sum(cached, axis=-1, keepdims=True) + jnp.sum(fresh, axis=-1, keepdims=True)
    dims = (((2,), (1,)), ((0,), (0,)))
    mixed = lax.dot_general(cached.astype(BF16), v_ref[0], dims, preferred_element_type=F32)
    mixed += lax.dot_general(fresh.astype(BF16), nv_ref[...], dims, preferred_element_type=F32)
    out_ref[...] = (mixed / total).astype(BF16)


def attend(query, cache, fresh, lengths, steps):
    requests, rows, size = query.shape
    length = cache.shape[2]
    pad = fresh.shape[2]
    block = 8

    def spec(which, n):
        return pl.BlockSpec((1, block, n, size), lambda i: (which, i, 0, 0))

    def plain(n):
        return pl.BlockSpec((block, n, size), lambda i: (i, 0, 0))

    return pl.pallas_call(
        functools.partial(attend_kernel, steps),
        grid=(requests // block,),
        out_shape=jax.ShapeDtypeStruct(query.shape, BF16),
        in_specs=[
            plain(rows),
            spec(0, length),
            spec(1, length),
            plain(pad),
            plain(pad),
            plain(1),
        ],
        out_specs=plain(rows),
        compiler_params=pltpu.CompilerParams(vmem_limit_bytes=32 * 2**20),
    )(query, cache, cache, fresh[0], fresh[1], lengths)


def per_device(line, hidden, weight, down, up, cache, step_kv, valid, adapters, pool):
    steps, requests, width = hidden.shape
    table = jnp.arange(pool.shape[0], dtype=jnp.int32)
    position = jnp.sum(jnp.where(adapters[:, None] == table[None, :], pool[None, :], 0), axis=1)
    position = jnp.broadcast_to(position[:, None], (requests, 2 * ADAPTER_RANK))
    query = project(hidden.reshape(steps * requests, width), weight, down, up, position, line)
    heads = weight.shape[1] // HEAD_SIZE
    query = query.reshape(steps, requests, heads, HEAD_SIZE).transpose(1, 0, 2, 3)
    fresh = jnp.pad(step_kv.transpose(1, 2, 0, 3), ((0, 0), (0, 0), (0, 16 - steps), (0, 0)))
    lengths = jnp.broadcast_to(valid[:, None, None], (requests, 1, HEAD_SIZE))
    out = attend(
        query.reshape(requests, steps * heads, HEAD_SIZE), cache, fresh, lengths, steps
    )
    out = out.reshape(requests, steps, heads * HEAD_SIZE)
    return out.transpose(1, 0, 2)


def solution(mesh):
    return jax.shard_map(
        functools.partial(per_device, mesh.shape["dp"] // 2),
        mesh=mesh,
        in_specs=(
            P(None, "dp", "tensor"),
            P(None, "tensor"),
            P("dp", "tensor"),
            P("dp", "tensor"),
            P(None, "dp", None, "tensor"),
            P(None, None, "dp", "tensor"),
            P("dp"),
            P("dp"),
            P(),
        ),
        out_specs=P(None, "dp", "tensor"),
        check_vma=False,
    )
```
